512 devices in a mesh: occ: 32 (over z, x_lo), aux: 16 (over x_hi, y, core).
Axes of the slice: x: 4 (x_hi: 2, x_lo: 2; x = x_hi * 2 + x_lo), y: 4, z: 16, core: 2. Of those that a mesh axis runs over, the one named last changes fastest.
Arguments:
- orbital_factors: bfloat16 [64, 256, 20480], P('occ', None, 'aux'), may hold values from -0.41992188 to 0.41992188
- occ_energy: bfloat16 [64], P('occ'), may hold values from -2 to -0.5
- vir_energy: float32 [256], replicated, may hold values from 0.5 to 3
- pair_kept: int32 [32, 2], P('occ'), may hold values 0 or 1
Outputs:
- gamma: float32 [64, 256, 20480], P('occ', None, 'aux')
The draws below stay inside these ranges and needn't reach their ends.
All inputs are finite; a program needn't handle non-finite values. No bound on the sum of `pair_kept` on one device may be relied on, other than what follows from the above.
Results may differ from the reference program's by a relative error of at most 0.0034.
Values may be sent and summed in bfloat16 or wider, within the bound.
A program may use at most 64 MiB of HBM per device.

```python
import jax
import jax.numpy as jnp
from jax import lax

OCC_DEV = 2
VS = 256
ROUNDS = 2
NOCC = 64
NAUX = 20480
N_OCC = 32


def plant(values, rng, least, high):
    longest = values.shape.index(max(values.shape))
    spots = []
    for shift in (0, 1):
        where = [jax.random.randint(jax.random.fold_in(rng, axis), (), 0, length) for axis, length in enumerate(values.shape)]
        where[longest] = (where[longest] + shift) % values.shape[longest]
        spots.append(tuple(where))
    return values.at[spots[0]].set(least).at[spots[1]].set(high)


def levels(own_key, dims, shards, least, top_value):
    def one(dim, shards_of):
        heights = jax.random.uniform(jax.random.fold_in(jax.random.fold_in(own_key, 6), dim), (shards_of,), jnp.float32, least / len(shards), top_value / len(shards))
        return jnp.repeat(jnp.exp(heights), dims[dim] // shards_of).reshape((-1,) + (1,) * (len(dims) - dim - 1))

    loudness = one(*shards[0])
    for cut in shards[1:]:
        loudness = loudness * one(*cut)
    return loudness


def normal_values(rng, extent, deviation, most, cuts=(), held_as=jnp.bfloat16):
    gain = levels(rng, extent, cuts, -0.22, 0.18) if cuts else 1.0
    array = jax.random.normal(rng, extent, jnp.float32) * deviation * gain
    return jnp.minimum(jnp.maximum(array, -most), most).astype(held_as)


def setup_inputs(seed: int = 0) -> dict:
    arg_keys = jax.random.split(jax.random.key(seed), 5)
    orbital_factors = normal_values(arg_keys[0], (NOCC, VS, NAUX), 0.07, 0.41992188, ((0, 32), (2, 16)))
    occ_energy = jnp.clip(-2.0 + 1.5 * jax.random.uniform(arg_keys[1], (NOCC,), jnp.float32) ** levels(arg_keys[1], (NOCC,), ((0, 32),), -0.2, 0.2), -2.0, -0.5).astype(jnp.bfloat16)
    vir_energy = jnp.clip(jax.random.uniform(arg_keys[2], (VS,), jnp.float32, 0.5, 3.0), 0.5, 3.0)
    pair_kept = plant((jax.random.randint(arg_keys[3], (N_OCC, ROUNDS), 0, 3) < 2).astype(jnp.int32), jax.random.fold_in(arg_keys[3], 1), 0, 1)
    return dict(orbital_factors=orbital_factors, occ_energy=occ_energy, vir_energy=vir_energy, pair_kept=pair_kept)


def pair_amplitudes(own_rows, partner_rows, own_e, partner_e, vir_e, flag):
    product = jnp.dot(own_rows, partner_rows.T, preferred_element_type=jnp.float32)
    blocks = product.reshape(OCC_DEV, VS, OCC_DEV, VS)
    mixed = 2.0 * blocks - jnp.transpose(blocks, (0, 3, 2, 1))
    denom = own_e[:, None, None, None] + partner_e[None, None, :, None] - vir_e[None, :, None, None] - vir_e[None, None, None, :]
    return (flag * mixed / denom).astype(jnp.bfloat16).reshape(OCC_DEV * VS, OCC_DEV * VS)


def reference(orbital_factors, occ_energy, vir_energy, pair_kept):
    width = OCC_DEV * VS
    all_rows = orbital_factors.reshape(NOCC * VS, NAUX)
    occ_e = occ_energy.astype(jnp.float32)
    vir_e = vir_energy.astype(jnp.float32)
    gamma = jnp.zeros((NOCC * VS, NAUX), jnp.float32)
    for offset_step in range(ROUNDS):
        def visit(block, gamma):
            block = jnp.asarray(block).astype(jnp.int32)
            partner = ((block + offset_step + 1) % N_OCC).astype(jnp.int32)
            own_rows = lax.dynamic_slice_in_dim(all_rows, block * width, width, 0)
            partner_rows = lax.dynamic_slice_in_dim(all_rows, partner * width, width, 0)
            own_e = lax.dynamic_slice_in_dim(occ_e, block * OCC_DEV, OCC_DEV, 0)
            partner_e = lax.dynamic_slice_in_dim(occ_e, partner * OCC_DEV, OCC_DEV, 0)
            flag = pair_kept[block, offset_step].astype(jnp.float32)
            tilde = pair_amplitudes(own_rows, partner_rows, own_e, partner_e, vir_e, flag)
            own_term = jnp.dot(tilde, partner_rows, preferred_element_type=jnp.float32)
            back_term = lax.dot_general(tilde, own_rows, (((0,), (0,)), ((), ())), preferred_element_type=jnp.float32)
            back_term = lax.optimization_barrier(back_term.astype(jnp.bfloat16)).astype(jnp.float32)
            current = lax.dynamic_slice_in_dim(gamma, block * width, width, 0)
            gamma = lax.dynamic_update_slice_in_dim(gamma, current + own_term, block * width, 0)
            current = lax.dynamic_slice_in_dim(gamma, partner * width, width, 0)
            gamma = lax.dynamic_update_slice_in_dim(gamma, current + back_term, partner * width, 0)
            return gamma

        gamma = lax.fori_loop(0, N_OCC, visit, gamma)
    return gamma.reshape(NOCC, VS, NAUX)
```

```python
import functools

import jax
import jax.numpy as jnp
from jax import lax
from jax.experimental import pallas as pl
from jax.experimental.pallas import tpu as pltpu
from jax.sharding import PartitionSpec as P

F32 = jnp.float32
BF16 = jnp.bfloat16
NT = (((1,), (1,)), ((), ()))

X, F, R, D, ME = range(5)
KINDS = ((ME, X), (X, F), (ME, F), (R, ME))
PAIRS = ((ME, X), (ME, F), (R, ME), (D, ME))


def kernel(
    planes, b_hbm, small_ref, out_hbm,
    bb, small, k, rc, ry, rx, cx, cr, cf, t, tt, g,
    send, recv, local, out_sem,
):
    slab = k.shape[1]
    rows = slab // 16
    half = b_hbm.shape[1] // 2

    occ, aux = lax.axis_index("occ"), lax.axis_index("aux")
    z, lo = occ // 2, lax.rem(occ, 2)
    core, y, xh = lax.rem(aux, 2), lax.rem(aux // 2, 4), aux // 8
    ahead = lax.rem(z + planes + 1 - 2 * lo, planes)
    behind = lax.rem(z + planes - 1 + 2 * lo, planes)
    occ_of = (z * 2 + 1 - lo, ahead * 2 + lo, behind * 2 + lo, behind * 2 + 1 - lo)

    def aux_of(xh_, y_, core_):
        return (xh_ * 4 + y_) * 2 + core_

    y1, y2, y3 = y + 1 - 2 * lax.rem(y, 2), lax.rem(y + 2, 4), 3 - y
    other_core, other_xh = 1 - core, 1 - xh
    to_core = (occ, aux_of(xh, y, other_core))
    to_y1 = (occ, aux_of(xh, y1, core))
    to_y3 = (occ, aux_of(xh, y3, core))
    to_xh = (occ, aux_of(other_xh, y, core))
    to = [(o, aux) for o in occ_of]

    def device(where):
        return {"occ": where[0], "aux": where[1]}

    def copy(n, src, dst, where):
        return pltpu.make_async_remote_copy(
            src_ref=src, dst_ref=dst, send_sem=send.at[n], recv_sem=recv.at[n],
            device_id=device(where), device_id_type=pl.DeviceIdType.MESH,
        )

    own = pltpu.make_async_copy(b_hbm, bb.at[ME], local.at[0])
    own.start()
    barrier = pltpu.get_barrier_semaphore()
    for where in (*to, to_core, to_y1, to_y3, to_xh):
        pl.semaphore_signal(barrier, inc=1, device_id=device(where), device_id_type=pl.DeviceIdType.MESH)
    pl.semaphore_wait(barrier, 8)

    mine = pl.ds(pl.multiple_of(half * (1 - lo), half), half)
    others = pl.ds(pl.multiple_of(half * lo, half), half)

    started = []

    def start(*args):
        c = copy(*args)
        c.start()
        started.append(c)
        return c

    first_x = start(0, b_hbm.at[:, others], bb.at[X, :, others], to[X])
    first_f = start(1, b_hbm.at[:, mine], bb.at[F, :, mine], to[R])
    first_r = start(2, b_hbm.at[:, others], bb.at[R, :, others], to[F])
    smalls = [
        start(8 + slot, small_ref.at[pl.ds(rows, 8)], small.at[slot], to[back])
        for slot, back in ((X, X), (F, R), (R, F), (D, D))
    ]

    def pair_sums(kind, columns):
        p, q = KINDS[kind]
        first, second = p + lo * (q - p), q + lo * (p - q)

        def block(i, j):
            a = bb[first, i * slab:(i + 1) * slab, columns]
            b = bb[second, j * slab:(j + 1) * slab, columns]
            direct = lax.dot_general(a + a, b, NT, preferred_element_type=F32)
            exchanged = lax.dot_general(b, a, NT, preferred_element_type=F32)
            k[2 * kind + i, :, j * slab:(j + 1) * slab] = direct - exchanged

        for i in range(2):
            for j in range(2):
                block(i, j)

    own.wait()
    first_x.wait_recv()
    pair_sums(0, mine)
    first_f.wait_recv()
    second = [
        start(3, bb.at[X, :, mine], bb.at[D, :, mine], to[F]),
        start(4, bb.at[F, :, mine], bb.at[D, :, mine], to[X]),
    ]
    first_r.wait_recv()
    second += [
        start(5, b_hbm.at[:, mine], bb.at[X, :, mine], to[X]),
        start(6, b_hbm.at[:, others], bb.at[F, :, others], to[R]),
        start(7, b_hbm.at[:, mine], bb.at[R, :, mine], to[F]),
    ]
    pair_sums(1, mine)
    pair_sums(2, mine)
    pair_sums(3, others)

    def rows_of(core_, y_, xh_):
        c = core_ * 8 + y_ * 2 + xh_
        return pl.ds(pl.multiple_of(c * rows, rows), rows)

    def part(core_, y_, xh_):
        return k.at[:, rows_of(core_, y_, xh_)]

    def add(core_, y_, xh_, got):
        r = rows_of(core_, y_, xh_)
        k[:, r, :] = k[:, r, :] + got[...]

    n = 12
    stage = []
    for y_ in range(4):
        for x_ in range(2):
            stage.append((start(n, part(other_core, y_, x_), rc.at[y_ * 2 + x_], to_core), y_, x_))
            n += 1
    for c, y_, x_ in stage:
        c.wait_recv()
        add(core, y_, x_, rc.at[y_ * 2 + x_])

    one = [
        start(20, part(core, y2, 0), ry.at[0], to_y1),
        start(21, part(core, y2, 1), ry.at[1], to_y3),
        start(22, part(core, y1, 0), ry.at[2], to_y1),
        start(23, part(core, y3, 1), ry.at[3], to_y3),
    ]
    one[0].wait_recv()
    add(core, y3, 0, ry.at[0])
    two = [start(24, part(core, y3, 0), ry.at[4], to_y3)]
    one[1].wait_recv()
    add(core, y1, 1, ry.at[1])
    two.append(start(25, part(core, y1, 1), ry.at[5], to_y1))
    one[2].wait_recv()
    add(core, y, 0, ry.at[2])
    one[3].wait_recv()
    add(core, y, 1, ry.at[3])
    two[0].wait_recv()
    add(core, y, 0, ry.at[4])
    two[1].wait_recv()
    add(core, y, 1, ry.at[5])
    across = start(26, part(core, y, other_xh), rx, to_xh)
    across.wait_recv()
    add(core, y, xh, rx)

    mine_r = rows_of(core, y, xh)
    from_x = start(27, k.at[0:4, mine_r], cx, to[X])
    from_r = start(28, k.at[2:6, mine_r], cr, to[F])
    from_f = start(29, k.at[6:8, mine_r], cf, to[R])
    for c in smalls:
        c.wait_recv()
    small[ME] = small_ref[rows:rows + 8]
    from_x.wait_recv()
    from_r.wait_recv()
    from_f.wait_recv()
    totals = (
        lambda i: k[i, mine_r, :] + cx[i],
        lambda i: k[4 + i, mine_r, :] + cf[i],
        lambda i: k[6 + i, mine_r, :] + cr[2 + i],
        lambda i: cx[2 + i] + cr[i],
    )
    virtual = small_ref[0:rows]
    for pair, (p, q) in enumerate(PAIRS):
        first, second_ = p + lo * (q - p), q + lo * (p - q)
        flag_row = 2 + (0 if pair in (X, D) else 1)
        flag = small[first, flag_row:flag_row + 1]
        for i in range(2):
            total = totals[pair](i)
            for j in range(2):
                at = slice(j * slab, (j + 1) * slab)
                energy = small[first, i:i + 1] + small[second_, j:j + 1]
                t[2 * pair + i, mine_r, at] = (flag * total[:, at] / (energy - virtual)).astype(BF16)

    def rows_t(core_, y_, xh_):
        return t.at[:, rows_of(core_, y_, xh_)]

    def spread(n, core_, y_, xh_, where):
        return start(n, rows_t(core_, y_, xh_), rows_t(core_, y_, xh_), where)

    base = 30
    got = [spread(base, core, y, xh, to_xh)]
    a0 = spread(base + 1, core, y, xh, to_y3)
    b0 = spread(base + 2, core, y, xh, to_y1)
    s0 = spread(base + 3, core, y, xh, to_core)
    got[0].wait_recv()
    s1 = spread(base + 4, core, y, other_xh, to_core)
    a1 = spread(base + 5, core, y, other_xh, to_y3)
    b1 = spread(base + 6, core, y, other_xh, to_y1)
    a0.wait_recv()
    a2 = spread(base + 7, core, y3, xh, to_y1)
    s2 = spread(base + 8, core, y3, xh, to_core)
    b0.wait_recv()
    s3 = spread(base + 9, core, y1, xh, to_core)
    a1.wait_recv()
    s4 = spread(base + 10, core, y3, other_xh, to_core)
    b1.wait_recv()
    b2 = spread(base + 11, core, y1, other_xh, to_y3)
    s5 = spread(base + 12, core, y1, other_xh, to_core)
    a2.wait_recv()
    s6 = spread(base + 13, core, y2, xh, to_core)
    b2.wait_recv()
    s7 = spread(base + 14, core, y2, other_xh, to_core)
    for c in (s0, s1, s2, s3, s4, s5, s6, s7):
        c.wait_recv()

    turned = 2 * (1 - lo)
    straight = 2 * lo
    for u in range(2):
        for i in range(2):
            for j in range(2):
                block = t[2 * (turned + u) + i, :, j * slab:(j + 1) * slab]
                tt[2 * u + j, :, i * slab:(i + 1) * slab] = block.T

    for c in second:
        c.wait_recv()
    width = g.shape[2]
    results = []
    for s in range(2 * half // width):
        at = slice(s * width, (s + 1) * width)
        for i in range(2):
            total = jnp.zeros((slab, width), F32)
            for u in range(2):
                total += jnp.dot(t[2 * (straight + u) + i], bb[straight + u, :, at], preferred_element_type=F32)
                total += jnp.dot(tt[2 * u + i], bb[turned + u, :, at], preferred_element_type=F32)
            g[s, i * slab:(i + 1) * slab] = total
        result = pltpu.make_async_copy(g.at[s], out_hbm.at[:, at], out_sem.at[s])
        result.start()
        results.append(result)
    for c in started:
        c.wait_send()
    for c in results:
        c.wait()


def on_device(planes, orbital_factors, occ_energy, vir_energy, pair_kept):
    occ_dev, slab, aux_dev = orbital_factors.shape
    width = occ_dev * slab
    rows = slab // 16
    chunks = 5 if aux_dev % 640 == 0 else 2
    aux = lax.axis_index("aux")
    c = lax.rem(aux, 2) * 8 + lax.rem(aux // 2, 4) * 2 + aux // 8
    mine = lax.dynamic_slice_in_dim(vir_energy, c * rows, rows, 0)
    virtual = mine[:, None] + vir_energy[None, :]
    scalars = jnp.concatenate([occ_energy.astype(F32), pair_kept[0].astype(F32), jnp.zeros((4,), F32)])
    small = jnp.concatenate([virtual, jnp.broadcast_to(scalars[:, None], (8, slab))])
    copies = 45
    gamma = pl.pallas_call(
        functools.partial(kernel, planes),
        out_shape=jax.ShapeDtypeStruct((width, aux_dev), F32),
        in_specs=[pl.BlockSpec(memory_space=pl.ANY), pl.BlockSpec(memory_space=pltpu.VMEM)],
        out_specs=pl.BlockSpec(memory_space=pl.ANY),
        scratch_shapes=[
            pltpu.VMEM((5, width, aux_dev), BF16),
            pltpu.VMEM((5, 8, slab), F32),
            pltpu.VMEM((8, slab, width), F32),
            pltpu.VMEM((8, 8, rows, width), F32),
            pltpu.VMEM((6, 8, rows, width), F32),
            pltpu.VMEM((8, rows, width), F32),
            pltpu.VMEM((4, rows, width), F32),
            pltpu.VMEM((4, rows, width), F32),
            pltpu.VMEM((2, rows, width), F32),
            pltpu.VMEM((8, slab, width), BF16),
            pltpu.VMEM((4, slab, width), BF16),
            pltpu.VMEM((chunks, width, aux_dev // chunks), F32),
            pltpu.SemaphoreType.DMA((copies,)),
            pltpu.SemaphoreType.DMA((copies,)),
            pltpu.SemaphoreType.DMA((1,)),
            pltpu.SemaphoreType.DMA((chunks,)),
        ],
        compiler_params=pltpu.CompilerParams(
            collective_id=0, has_side_effects=True, vmem_limit_bytes=48 * 1024 * 1024
        ),
        cost_estimate=pl.CostEstimate(
            flops=12 * width * width * aux_dev, bytes_accessed=6 * width * aux_dev, transcendentals=0
        ),
    )(orbital_factors.reshape(width, aux_dev), small)
    return gamma.reshape(occ_dev, slab, aux_dev)


def solution(mesh):
    in_specs = (P("occ", None, "aux"), P("occ"), P(), P("occ", None))
    out_specs = P("occ", None, "aux")
    return jax.shard_map(
        functools.partial(on_device, mesh.shape["occ"] // 2),
        mesh=mesh, in_specs=in_specs, out_specs=out_specs, check_vma=False,
    )
```

```python
import functools

import jax
import jax.numpy as jnp
from jax import lax
from jax.experimental import pallas as pl
from jax.experimental.pallas import tpu as pltpu
from jax.sharding import PartitionSpec as P

F32 = jnp.float32
BF16 = jnp.bfloat16
I16 = jnp.int16
TOP = 32760.0
NT = (((1,), (1,)), ((), ()))

X, F, R, D, ME = range(5)
KINDS = ((ME, X), (X, F), (ME, F), (ME, R))
KX, KXF, KF, KR = range(4)
BATCHES = (
    ((KX, 0, 0), (KX, 1, 0), (KXF, 0, 0), (KF, 0, 0), (KF, 1, 0), (KR, 0, 0), (KR, 1, 0)),
    ((KX, 0, 1), (KX, 1, 1), (KXF, 0, 1), (KXF, 1, 0), (KXF, 1, 1), (KF, 0, 1), (KF, 1, 1), (KR, 0, 1), (KR, 1, 1)),
)
BLOCKS = BATCHES[0] + BATCHES[1]
AT = {block: n for n, block in enumerate(BLOCKS)}
SPANS = ((0, 7), (7, 16))
TO_X = ((0, 3), (7, 12))
TO_F = ((2, 5), (9, 14))
TO_R = ((5, 7), (14, 16))
CUT = (3, 12)
SCALES = ((0, 8), (8, 24))


def kernel(
    planes, b_hbm, e_ref, v_ref, kept_ref, out_hbm,
    bb, small, k, rc, q, scale, ry, ry_scale, ys, rx, p, cx, cr, cf, t, tt, g,
    send, recv, local, out_sem,
):
    slab = k.shape[1]
    rows, yrows, crows = slab // 16, slab // 8, slab // 2
    half = b_hbm.shape[1] // 2

    occ, aux = lax.axis_index("occ"), lax.axis_index("aux")
    z, lo = occ // 2, lax.rem(occ, 2)
    core, y, xh = lax.rem(aux, 2), lax.rem(aux // 2, 4), aux // 8
    ahead = lax.rem(z + planes + 1 - 2 * lo, planes)
    behind = lax.rem(z + planes - 1 + 2 * lo, planes)
    occ_of = (z * 2 + 1 - lo, ahead * 2 + lo, behind * 2 + lo, behind * 2 + 1 - lo)

    def aux_of(xh_, y_, core_):
        return (xh_ * 4 + y_) * 2 + core_

    y1, y2, y3 = y + 1 - 2 * lax.rem(y, 2), lax.rem(y + 2, 4), 3 - y
    other_core, other_xh = 1 - core, 1 - xh
    to_core = (occ, aux_of(xh, y, other_core))
    to_y = [(occ, aux_of(xh, y_, core)) for y_ in (y1, y2, y3)]
    to_xh = (occ, aux_of(other_xh, y, core))
    to = [(o, aux) for o in occ_of]

    def device(where):
        return {"occ": where[0], "aux": where[1]}

    started = []
    numbers = iter(range(send.shape[0]))

    def start(src, dst, where):
        n = next(numbers)
        c = pltpu.make_async_remote_copy(
            src_ref=src, dst_ref=dst, send_sem=send.at[n], recv_sem=recv.at[n],
            device_id=device(where), device_id_type=pl.DeviceIdType.MESH,
        )
        c.start()
        started.append(c)
        return c

    own = pltpu.make_async_copy(b_hbm, bb.at[ME], local.at[0])
    own.start()
    barrier = pltpu.get_barrier_semaphore()
    for where in (*to, to_core, *to_y, to_xh):
        pl.semaphore_signal(barrier, inc=1, device_id=device(where), device_id_type=pl.DeviceIdType.MESH)

    for i in range(2):
        small[ME, i:i + 1] = jnp.broadcast_to(e_ref[:, i:i + 1].astype(F32), (1, slab))
        small[ME, 2 + i:3 + i] = jnp.broadcast_to(kept_ref[:, i:i + 1].astype(F32), (1, slab))
    small[ME, 4:8] = jnp.zeros((4, slab), F32)
    my_row = core * crows + y * yrows + xh * rows
    spot = lax.broadcasted_iota(jnp.int32, (rows, slab), 1) - lax.broadcasted_iota(jnp.int32, (rows, slab), 0)
    mine_v = jnp.sum(jnp.where(spot == my_row, v_ref[...], 0.0), axis=1, keepdims=True)
    virtual = mine_v + v_ref[...]

    pl.semaphore_wait(barrier, 9)

    mine = pl.ds(pl.multiple_of(half * (1 - lo), half), half)
    others = pl.ds(pl.multiple_of(half * lo, half), half)

    lo_mine, lo_others = half * (1 - lo), half * lo
    cut = half * 2 // 5

    def columns_at(first_, count):
        return pl.ds(pl.multiple_of(first_, 128), count)

    def forward(slot, first_, count, where):
        c = columns_at(first_, count)
        return start(bb.at[slot, :, c], bb.at[D, :, c], to[where])

    first = []
    for o in range(2):
        r = slice(o * slab, (o + 1) * slab)
        first.append((
            start(b_hbm.at[r, others], bb.at[X, r, others], to[X]),
            start(b_hbm.at[r, mine], bb.at[F, r, mine], to[R]),
            start(b_hbm.at[r, others], bb.at[R, r, others], to[F]),
        ))
    smalls = [
        start(small.at[ME], small.at[slot], to[back])
        for slot, back in ((X, X), (F, R), (R, F), (D, D))
    ]

    def pair_sums(lo_, hi_):
        for n in range(lo_, hi_):
            kind, u, v = BLOCKS[n]
            one, two = KINDS[kind]
            swap = 1 - lo if kind == KR else lo
            columns = others if kind == KR else mine
            head, tail = one + swap * (two - one), two + swap * (one - two)
            a_at = pl.multiple_of((u + swap * (v - u)) * slab, slab)
            b_at = pl.multiple_of((v + swap * (u - v)) * slab, slab)
            a = bb[head, pl.ds(a_at, slab), columns]
            b = bb[tail, pl.ds(b_at, slab), columns]
            direct = lax.dot_general(a + a, b, NT, preferred_element_type=F32)
            exchanged = lax.dot_general(b, a, NT, preferred_element_type=F32)
            k[n] = direct - exchanged

    my_half = pl.ds(pl.multiple_of(core * crows, crows), crows)
    its_half = pl.ds(pl.multiple_of(other_core * crows, crows), crows)

    def to_other_core(lo_, hi_):
        return start(k.at[lo_:hi_, its_half], rc.at[lo_:hi_], to_core)

    def sum_cores(lo_, hi_, shift):
        for n in range(lo_, hi_):
            total = k[n, my_half] + rc[n]
            k[n, my_half] = total
            top = jnp.max(jnp.max(jnp.abs(total), axis=0, keepdims=True), axis=1, keepdims=True)
            top = jnp.maximum(top, 1e-30)
            q[n] = jnp.round(total * (TOP / top)).astype(jnp.int32).astype(I16)
            scale[n + shift:n + shift + 1] = jnp.broadcast_to(top * (1.0 / TOP), (1, 128))

    def along_y(batch):
        lo_, hi_ = SPANS[batch]
        s_lo, s_hi = SCALES[batch]
        out = []
        for j, y_ in enumerate((y1, y2, y3)):
            r = pl.ds(pl.multiple_of(y_ * yrows, yrows), yrows)
            out.append(start(scale.at[s_lo:s_hi], ry_scale.at[j, s_lo:s_hi], to_y[j]))
            out.append(start(q.at[lo_:hi_, r], ry.at[j, lo_:hi_], to_y[j]))
        return out

    def sum_y(batch, copies):
        for c in copies:
            c.wait_recv()
        lo_, hi_ = SPANS[batch]
        r = pl.ds(pl.multiple_of(core * crows + y * yrows, yrows), yrows)
        for n in range(lo_, hi_):
            total = k[n, r]
            for j in range(3):
                total += ry[j, n].astype(jnp.int32).astype(F32) * ry_scale[j, n + batch:n + batch + 1, 0:1]
            ys[n] = total
        x_rows = pl.ds(pl.multiple_of(other_xh * rows, rows), rows)
        return start(ys.at[lo_:hi_, x_rows], rx.at[lo_:hi_], to_xh)

    def sum_x(batch, c):
        c.wait_recv()
        lo_, hi_ = SPANS[batch]
        p[lo_:hi_] = ys[lo_:hi_, pl.ds(pl.multiple_of(xh * rows, rows), rows)] + rx[lo_:hi_]
        out = []
        for (a_, b_), dst, where in ((TO_X[batch], cx, to[X]), (TO_F[batch], cr, to[F]), (TO_R[batch], cf, to[R])):
            out.append(start(p.at[a_:b_], dst.at[a_:b_], where))
        return out

    own.wait()
    for c in first[0]:
        c.wait_recv()
    pair_sums(SPANS[0][0], CUT[0])
    core0 = [to_other_core(SPANS[0][0], CUT[0])]
    pair_sums(CUT[0], SPANS[0][1])
    core0.append(to_other_core(CUT[0], SPANS[0][1]))
    core0[0].wait_recv()
    sum_cores(SPANS[0][0], CUT[0], 0)
    core0[1].wait_recv()
    sum_cores(CUT[0], SPANS[0][1], 0)
    y_0 = along_y(0)
    for c in first[1]:
        c.wait_recv()
    second = [
        start(b_hbm.at[:, mine], bb.at[X, :, mine], to[X]),
        start(b_hbm.at[:, others], bb.at[F, :, others], to[R]),
        start(b_hbm.at[:, mine], bb.at[R, :, mine], to[F]),
    ]
    pair_sums(SPANS[1][0], CUT[1])
    core1 = [to_other_core(SPANS[1][0], CUT[1])]
    pair_sums(CUT[1], SPANS[1][1])
    core1.append(to_other_core(CUT[1], SPANS[1][1]))
    core1[0].wait_recv()
    sum_cores(SPANS[1][0], CUT[1], 1)
    core1[1].wait_recv()
    sum_cores(CUT[1], SPANS[1][1], 1)
    y_1 = along_y(1)
    x_0 = sum_y(0, y_0)
    x_1 = sum_y(1, y_1)
    place_0 = sum_x(0, x_0)
    diagonal = [forward(X, lo_mine, cut, F)]
    for c in smalls:
        c.wait_recv()
    place_1 = sum_x(1, x_1)
    for c in place_0 + place_1:
        c.wait_recv()

    second[0].wait_recv()
    diagonal += [forward(X, lo_mine + cut, half - cut, F), forward(X, lo_others, cut, F)]

    my_rows = pl.ds(pl.multiple_of(my_row, rows), rows)
    for pair in (X, F, R, D):
        swap = lo if pair in (X, F) else 1 - lo
        flag_row = 2 if pair in (X, D) else 3
        flag = small[ME + swap * (pair - ME), flag_row:flag_row + 1]
        for i in range(2):
            for j in range(2):
                if pair == X:
                    total = p[AT[KX, i, j]] + cx[AT[KX, j, i]]
                elif pair == F:
                    total = p[AT[KF, i, j]] + cf[AT[KR, j, i]]
                elif pair == R:
                    total = p[AT[KR, i, j]] + cr[AT[KF, j, i]]
                else:
                    total = cx[AT[KXF, i, j]] + cr[AT[KXF, j, i]]
                energy = small[ME, i:i + 1] + small[pair, j:j + 1]
                t[2 * pair + i, my_rows, j * slab:(j + 1) * slab] = (flag * total / (energy - virtual)).astype(BF16)

    to_y1, _, to_y3 = to_y

    def spread(part, core_, y_, xh_, where):
        r = pl.ds(pl.multiple_of(core_ * crows + y_ * yrows + xh_ * rows, rows), rows)
        source = t.at[4 * part:4 * part + 4, r]
        return start(source, source, where)

    own_part, near, far, last = [], [], [], []
    for h in range(2):
        own_part.append((
            spread(h, core, y, xh, to_xh),
            spread(h, core, y, xh, to_y3),
            spread(h, core, y, xh, to_y1),
            spread(h, core, y, xh, to_core),
        ))
    for h in range(2):
        own_part[h][0].wait_recv()
        near.append((
            spread(h, core, y, other_xh, to_y3),
            spread(h, core, y, other_xh, to_y1),
            spread(h, core, y, other_xh, to_core),
        ))
        own_part[h][1].wait_recv()
        far.append([spread(h, core, y3, xh, to_y1), spread(h, core, y3, xh, to_core)])
        own_part[h][2].wait_recv()
        far[h].append(spread(h, core, y1, xh, to_core))
    diagonal.append(forward(F, lo_mine + cut, half - cut, X))
    for h in range(2):
        near[h][1].wait_recv()
        far[h] += [spread(h, core, y1, other_xh, to_y3), spread(h, core, y1, other_xh, to_core)]
        near[h][0].wait_recv()
        far[h].append(spread(h, core, y3, other_xh, to_core))
    for h in range(2):
        far[h][0].wait_recv()
        last.append([spread(h, core, y2, xh, to_core)])
        far[h][3].wait_recv()
        last[h].append(spread(h, core, y2, other_xh, to_core))

    def orient(h):
        for c in (own_part[h][3], near[h][2], far[h][1], far[h][2], far[h][4], far[h][5], last[h][0], last[h][1]):
            c.wait_recv()

        @pl.when(lo == h)
        def _():
            tt[4 * h:4 * h + 4] = t[4 * h:4 * h + 4]

        @pl.when(lo != h)
        def _():
            for n in range(4 * h, 4 * h + 4):
                for j in range(2):
                    tt[n, :, j * slab:(j + 1) * slab] = t[n, :, j * slab:(j + 1) * slab].T

    pieces = ((lo_mine, cut), (lo_mine + cut, half - cut), (lo_others, cut), (lo_others + cut, half - cut))

    def apply(slots, piece, earlier):
        c = columns_at(*piece)
        out = []
        for i in range(2):
            total = earlier(i)
            for slot in slots:
                term = jnp.dot(tt[2 * slot + i], bb[slot, :, c], preferred_element_type=F32)
                total = term if total is None else total + term
            out.append(total)
        return out

    orient(0)
    second[1].wait_recv()
    at = 0
    for piece in pieces:
        for i, total in enumerate(apply((X, F), piece, lambda i: None)):
            g[i * slab:(i + 1) * slab, at:at + piece[1]] = total
        at += piece[1]
    orient(1)
    second[2].wait_recv()
    at = 0
    results = []
    for n, piece in enumerate(pieces):
        diagonal[n].wait_recv()
        here = slice(at, at + piece[1])
        for i, total in enumerate(apply((R, D), piece, lambda i: g[i * slab:(i + 1) * slab, here])):
            g[i * slab:(i + 1) * slab, here] = total
        result = pltpu.make_async_copy(g.at[:, here], out_hbm.at[:, columns_at(*piece)], out_sem.at[n])
        result.start()
        results.append(result)
        at += piece[1]
    for c in started:
        c.wait_send()
    for c in results:
        c.wait()


def on_device(planes, orbital_factors, occ_energy, vir_energy, pair_kept):
    occ_dev, slab, aux_dev = orbital_factors.shape
    width = occ_dev * slab
    rows = slab // 16
    copies = 72
    gamma = pl.pallas_call(
        functools.partial(kernel, planes),
        out_shape=jax.ShapeDtypeStruct((width, aux_dev), F32),
        in_specs=[pl.BlockSpec(memory_space=pltpu.HBM)] + [pl.BlockSpec(memory_space=pltpu.VMEM)] * 3,
        out_specs=pl.BlockSpec(memory_space=pl.ANY),
        scratch_shapes=[
            pltpu.VMEM((5, width, aux_dev), BF16),
            pltpu.VMEM((5, 8, slab), F32),
            pltpu.VMEM((16, slab, slab), F32),
            pltpu.VMEM((16, slab // 2, slab), F32),
            pltpu.VMEM((16, slab // 2, slab), I16),
            pltpu.VMEM((24, 128), F32),
            pltpu.VMEM((3, 16, slab // 8, slab), I16),
            pltpu.VMEM((3, 24, 128), F32),
            pltpu.VMEM((16, slab // 8, slab), F32),
            pltpu.VMEM((16, rows, slab), F32),
            pltpu.VMEM((16, rows, slab), F32),
            pltpu.VMEM((16, rows, slab), F32),
            pltpu.VMEM((16, rows, slab), F32),
            pltpu.VMEM((16, rows, slab), F32),
            pltpu.VMEM((8, slab, width), BF16),
            pltpu.VMEM((8, slab, width), BF16),
            pltpu.VMEM((width, aux_dev), F32),
            pltpu.SemaphoreType.DMA((copies,)),
            pltpu.SemaphoreType.DMA((copies,)),
            pltpu.SemaphoreType.DMA((1,)),
            pltpu.SemaphoreType.DMA((4,)),
        ],
        compiler_params=pltpu.CompilerParams(
            collective_id=0, has_side_effects=True, vmem_limit_bytes=60 * 1024 * 1024
        ),
        cost_estimate=pl.CostEstimate(
            flops=12 * width * width * aux_dev, bytes_accessed=6 * width * aux_dev, transcendentals=0
        ),
    )(orbital_factors.reshape(width, aux_dev), occ_energy.reshape(1, 2), vir_energy.reshape(1, slab), pair_kept)
    return gamma.reshape(occ_dev, slab, aux_dev)


def solution(mesh):
    in_specs = (P("occ", None, "aux"), P("occ"), P(), P("occ", None))
    out_specs = P("occ", None, "aux")
    return jax.shard_map(
        functools.partial(on_device, mesh.shape["occ"] // 2),
        mesh=mesh, in_specs=in_specs, out_specs=out_specs, check_vma=False,
    )
```

```python
import functools

import jax
import jax.numpy as jnp
from jax import lax
from jax.experimental import pallas as pl
from jax.experimental.pallas import tpu as pltpu
from jax.sharding import PartitionSpec as P

F32 = jnp.float32
BF16 = jnp.bfloat16
I16 = jnp.int16
TOP = 32760.0
NT = (((1,), (1,)), ((), ()))

X, F, R, D, ME = range(5)
KINDS = ((ME, X), (X, F), (ME, F), (ME, R))
KX, KXF, KF, KR = range(4)
BATCHES = (
    ((KX, 0, 0), (KX, 1, 0), (KXF, 0, 0), (KF, 0, 0), (KF, 1, 0), (KR, 0, 0), (KR, 1, 0)),
    ((KX, 0, 1), (KX, 1, 1), (KXF, 0, 1), (KXF, 1, 0), (KXF, 1, 1)),
    ((KF, 0, 1), (KF, 1, 1), (KR, 0, 1), (KR, 1, 1)),
)
BLOCKS = BATCHES[0] + BATCHES[1] + BATCHES[2]
AT = {block: n for n, block in enumerate(BLOCKS)}
SPANS = ((0, 7), (7, 12), (12, 16))
TO_X = ((0, 3), (7, 12), None)
TO_F = ((2, 5), (9, 12), (12, 14))
TO_R = ((5, 7), None, (14, 16))
ORDER = (X, D, F, R)


def kernel(
    planes, b_hbm, e_hbm, v_hbm, kept_hbm, out_hbm,
    bb, e_ref, v_ref, kept_ref, small, k, rc, q, scale, ry, ry_scale, ys, rx, p, cx, cr, cf, t, tt, g,
    send, recv, local, out_sem,
):
    slab = k.shape[1]
    rows, yrows, crows = slab // 16, slab // 8, slab // 2
    half = b_hbm.shape[1] // 2

    occ, aux = lax.axis_index("occ"), lax.axis_index("aux")
    z, lo = occ // 2, lax.rem(occ, 2)
    core, y, xh = lax.rem(aux, 2), lax.rem(aux // 2, 4), aux // 8
    ahead = lax.rem(z + planes + 1 - 2 * lo, planes)
    behind = lax.rem(z + planes - 1 + 2 * lo, planes)
    occ_of = (z * 2 + 1 - lo, ahead * 2 + lo, behind * 2 + lo, behind * 2 + 1 - lo)

    def aux_of(xh_, y_, core_):
        return (xh_ * 4 + y_) * 2 + core_

    y1, y2, y3 = y + 1 - 2 * lax.rem(y, 2), lax.rem(y + 2, 4), 3 - y
    other_core, other_xh = 1 - core, 1 - xh
    to_core = (occ, aux_of(xh, y, other_core))
    to_y = [(occ, aux_of(xh, y_, core)) for y_ in (y1, y2, y3)]
    to_xh = (occ, aux_of(other_xh, y, core))
    to = [(o, aux) for o in occ_of]

    def device(where):
        return {"occ": where[0], "aux": where[1]}

    started = []
    numbers = iter(range(send.shape[0]))

    def start(src, dst, where):
        n = next(numbers)
        c = pltpu.make_async_remote_copy(
            src_ref=src, dst_ref=dst, send_sem=send.at[n], recv_sem=recv.at[n],
            device_id=device(where), device_id_type=pl.DeviceIdType.MESH,
        )
        c.start()
        started.append(c)
        return c

    own = pltpu.make_async_copy(b_hbm, bb.at[ME], local.at[0])
    own.start()
    arguments = [
        pltpu.make_async_copy(src, dst, local.at[1 + n])
        for n, (src, dst) in enumerate(((e_hbm, e_ref), (v_hbm, v_ref), (kept_hbm, kept_ref)))
    ]
    for c in arguments:
        c.start()
    barrier = pltpu.get_barrier_semaphore()
    for where in (*to, to_core, *to_y, to_xh):
        pl.semaphore_signal(barrier, inc=1, device_id=device(where), device_id_type=pl.DeviceIdType.MESH)

    pl.semaphore_wait(barrier, 9)

    mine = pl.ds(pl.multiple_of(half * (1 - lo), half), half)
    others = pl.ds(pl.multiple_of(half * lo, half), half)

    lo_mine, lo_others = half * (1 - lo), half * lo
    cut = half * 2 // 5
    rest = half - cut

    def columns_at(first_, count):
        return pl.ds(pl.multiple_of(first_, 128), count)

    def forward(slot, first_, count, where):
        c = columns_at(first_, count)
        return start(bb.at[slot, :, c], bb.at[D, :, c], to[where])

    first = []
    for o in range(2):
        r = slice(o * slab, (o + 1) * slab)
        first.append((
            start(b_hbm.at[r, others], bb.at[X, r, others], to[X]),
            start(b_hbm.at[r, mine], bb.at[F, r, mine], to[R]),
            start(b_hbm.at[r, others], bb.at[R, r, others], to[F]),
        ))
    second = [
        start(b_hbm.at[:, mine], bb.at[X, :, mine], to[X]),
        start(b_hbm.at[:, others], bb.at[F, :, others], to[R]),
        start(b_hbm.at[:, mine], bb.at[R, :, mine], to[F]),
    ]

    for c in arguments:
        c.wait()
    for i in range(2):
        small[ME, i:i + 1] = jnp.broadcast_to(e_ref[:, i:i + 1].astype(F32), (1, slab))
        small[ME, 2 + i:3 + i] = jnp.broadcast_to(kept_ref[:, i:i + 1].astype(F32), (1, slab))
    small[ME, 4:8] = jnp.zeros((4, slab), F32)
    my_row = core * crows + y * yrows + xh * rows
    spot = lax.broadcasted_iota(jnp.int32, (rows, slab), 1) - lax.broadcasted_iota(jnp.int32, (rows, slab), 0)
    mine_v = jnp.sum(jnp.where(spot == my_row, v_ref[...], 0.0), axis=1, keepdims=True)
    virtual = mine_v + v_ref[...]

    smalls = [
        start(small.at[ME], small.at[slot], to[back])
        for slot, back in ((X, X), (F, R), (R, F), (D, D))
    ]

    def pair_sums(lo_, hi_):
        for n in range(lo_, hi_):
            kind, u, v = BLOCKS[n]
            one, two = KINDS[kind]
            swap = 1 - lo if kind == KR else lo
            columns = others if kind == KR else mine
            head, tail = one + swap * (two - one), two + swap * (one - two)
            a_at = pl.multiple_of((u + swap * (v - u)) * slab, slab)
            b_at = pl.multiple_of((v + swap * (u - v)) * slab, slab)
            a = bb[head, pl.ds(a_at, slab), columns]
            b = bb[tail, pl.ds(b_at, slab), columns]
            direct = lax.dot_general(a + a, b, NT, preferred_element_type=F32)
            exchanged = lax.dot_general(b, a, NT, preferred_element_type=F32)
            k[n] = direct - exchanged

    my_half = pl.ds(pl.multiple_of(core * crows, crows), crows)
    its_half = pl.ds(pl.multiple_of(other_core * crows, crows), crows)

    def to_other_core(lo_, hi_):
        return start(k.at[lo_:hi_, its_half], rc.at[lo_:hi_], to_core)

    def sum_cores(batch, lo_, hi_):
        for n in range(lo_, hi_):
            total = k[n, my_half] + rc[n]
            k[n, my_half] = total
            top = jnp.max(jnp.max(jnp.abs(total), axis=0, keepdims=True), axis=1, keepdims=True)
            top = jnp.maximum(top, 1e-30)
            q[n] = jnp.round(total * (TOP / top)).astype(jnp.int32).astype(I16)
            row = 8 * batch + n - SPANS[batch][0]
            scale[row:row + 1] = jnp.broadcast_to(top * (1.0 / TOP), (1, 128))

    def along_y(batch):
        lo_, hi_ = SPANS[batch]
        s = slice(8 * batch, 8 * batch + 8)
        out = []
        for j, y_ in enumerate((y1, y2, y3)):
            r = pl.ds(pl.multiple_of(y_ * yrows, yrows), yrows)
            out.append(start(scale.at[s], ry_scale.at[j, s], to_y[j]))
            out.append(start(q.at[lo_:hi_, r], ry.at[j, lo_:hi_], to_y[j]))
        return out

    def sum_y(batch, copies):
        for c in copies:
            c.wait_recv()
        lo_, hi_ = SPANS[batch]
        r = pl.ds(pl.multiple_of(core * crows + y * yrows, yrows), yrows)
        for n in range(lo_, hi_):
            row = 8 * batch + n - lo_
            total = k[n, r]
            for j in range(3):
                total += ry[j, n].astype(jnp.int32).astype(F32) * ry_scale[j, row:row + 1, 0:1]
            ys[n] = total
        x_rows = pl.ds(pl.multiple_of(other_xh * rows, rows), rows)
        return start(ys.at[lo_:hi_, x_rows], rx.at[lo_:hi_], to_xh)

    def sum_x(batch, c):
        c.wait_recv()
        lo_, hi_ = SPANS[batch]
        p[lo_:hi_] = ys[lo_:hi_, pl.ds(pl.multiple_of(xh * rows, rows), rows)] + rx[lo_:hi_]
        out = []
        for span, dst, where in ((TO_X[batch], cx, to[X]), (TO_F[batch], cr, to[F]), (TO_R[batch], cf, to[R])):
            if span is not None:
                out.append(start(p.at[slice(*span)], dst.at[slice(*span)], where))
        return out

    own.wait()
    for c in first[0]:
        c.wait_recv()
    pair_sums(0, 3)
    core0 = [to_other_core(0, 3)]
    pair_sums(3, 7)
    core0.append(to_other_core(3, 7))
    core0[0].wait_recv()
    sum_cores(0, 0, 3)
    core0[1].wait_recv()
    sum_cores(0, 3, 7)
    y_0 = along_y(0)
    for c in first[1]:
        c.wait_recv()
    pair_sums(*SPANS[1])
    core1 = to_other_core(*SPANS[1])
    pair_sums(*SPANS[2])
    core2 = to_other_core(*SPANS[2])
    core1.wait_recv()
    sum_cores(1, *SPANS[1])
    y_1 = along_y(1)
    core2.wait_recv()
    sum_cores(2, *SPANS[2])
    y_2 = along_y(2)
    x_0 = sum_y(0, y_0)
    x_1 = sum_y(1, y_1)
    x_2 = sum_y(2, y_2)
    diagonal = [forward(X, lo_mine, cut, F)]
    place_0 = sum_x(0, x_0)
    place_1 = sum_x(1, x_1)
    place_2 = sum_x(2, x_2)

    second[0].wait_recv()
    diagonal += [forward(X, lo_mine + cut, rest, F), forward(X, lo_others, cut, F)]

    my_rows = pl.ds(pl.multiple_of(my_row, rows), rows)

    def finish(pair):
        swap = lo if pair in (X, F) else 1 - lo
        flag_row = 2 if pair in (X, D) else 3
        flag = small[ME + swap * (pair - ME), flag_row:flag_row + 1]
        for i in range(2):
            for j in range(2):
                if pair == X:
                    total = p[AT[KX, i, j]] + cx[AT[KX, j, i]]
                elif pair == F:
                    total = p[AT[KF, i, j]] + cf[AT[KR, j, i]]
                elif pair == R:
                    total = p[AT[KR, i, j]] + cr[AT[KF, j, i]]
                else:
                    total = cx[AT[KXF, i, j]] + cr[AT[KXF, j, i]]
                energy = small[ME, i:i + 1] + small[pair, j:j + 1]
                row = 2 * ORDER.index(pair) + i
                t[row, my_rows, j * slab:(j + 1) * slab] = (flag * total / (energy - virtual)).astype(BF16)

    to_y1, _, to_y3 = to_y

    def spread(part, core_, y_, xh_, where):
        r = pl.ds(pl.multiple_of(core_ * crows + y_ * yrows + xh_ * rows, rows), rows)
        source = t.at[4 * part:4 * part + 4, r]
        return start(source, source, where)

    own_part, near, far, last = [], [], [], []
    for c in smalls + place_0 + place_1:
        c.wait_recv()
    for h in range(2):
        if h == 1:
            for c in place_2:
                c.wait_recv()
        finish(ORDER[2 * h])
        finish(ORDER[2 * h + 1])
        own_part.append((
            spread(h, core, y, xh, to_xh),
            spread(h, core, y, xh, to_y3),
            spread(h, core, y, xh, to_y1),
            spread(h, core, y, xh, to_core),
        ))
    for h in range(2):
        own_part[h][0].wait_recv()
        near.append((
            spread(h, core, y, other_xh, to_y3),
            spread(h, core, y, other_xh, to_y1),
            spread(h, core, y, other_xh, to_core),
        ))
        own_part[h][1].wait_recv()
        far.append([spread(h, core, y3, xh, to_y1), spread(h, core, y3, xh, to_core)])
        own_part[h][2].wait_recv()
        far[h].append(spread(h, core, y1, xh, to_core))
    diagonal.append(forward(F, lo_mine + cut, rest, X))
    for h in range(2):
        near[h][1].wait_recv()
        far[h] += [spread(h, core, y1, other_xh, to_y3), spread(h, core, y1, other_xh, to_core)]
        near[h][0].wait_recv()
        far[h].append(spread(h, core, y3, other_xh, to_core))
    for h in range(2):
        far[h][0].wait_recv()
        last.append([spread(h, core, y2, xh, to_core)])
        far[h][3].wait_recv()
        last[h].append(spread(h, core, y2, other_xh, to_core))

    def orient(h):
        for c in (own_part[h][3], near[h][2], far[h][1], far[h][2], far[h][4], far[h][5], last[h][0], last[h][1]):
            c.wait_recv()

        for n in range(4 * h, 4 * h + 4):
            second_at = 1 if ORDER[n // 2] in (X, F) else 0

            @pl.when(lo != second_at)
            def _(n=n):
                tt[n] = t[n]

            @pl.when(lo == second_at)
            def _(n=n):
                for j in range(2):
                    tt[n, :, j * slab:(j + 1) * slab] = t[n, :, j * slab:(j + 1) * slab].T

    pieces = ((lo_mine, cut), (lo_mine + cut, rest), (lo_others, cut), (lo_others + cut, rest))

    def apply(slots, piece, earlier):
        c = columns_at(*piece)
        out = []
        for i in range(2):
            total = earlier(i)
            for slot in slots:
                term = jnp.dot(tt[2 * ORDER.index(slot) + i], bb[slot, :, c], preferred_element_type=F32)
                total = term if total is None else total + term
            out.append(total)
        return out

    orient(0)
    at = 0
    for n, piece in enumerate(pieces):
        if n < 2:
            diagonal[n].wait_recv()
        for i, total in enumerate(apply((X, D) if n < 2 else (X,), piece, lambda i: None)):
            g[i * slab:(i + 1) * slab, at:at + piece[1]] = total
        at += piece[1]
    orient(1)
    second[1].wait_recv()
    second[2].wait_recv()
    at = 0
    results = []
    for n, piece in enumerate(pieces):
        here = slice(at, at + piece[1])
        if n >= 2:
            diagonal[n].wait_recv()
        slots = (F, R) if n < 2 else (F, R, D)
        for i, total in enumerate(apply(slots, piece, lambda i: g[i * slab:(i + 1) * slab, here])):
            g[i * slab:(i + 1) * slab, here] = total
        result = pltpu.make_async_copy(g.at[:, here], out_hbm.at[:, columns_at(*piece)], out_sem.at[n])
        result.start()
        results.append(result)
        at += piece[1]
    for c in started:
        c.wait_send()
    for c in results:
        c.wait()


def on_device(planes, orbital_factors, occ_energy, vir_energy, pair_kept):
    occ_dev, slab, aux_dev = orbital_factors.shape
    width = occ_dev * slab
    rows = slab // 16
    copies = 79
    gamma = pl.pallas_call(
        functools.partial(kernel, planes),
        out_shape=jax.ShapeDtypeStruct((width, aux_dev), F32),
        in_specs=[pl.BlockSpec(memory_space=pl.ANY)] * 4,
        out_specs=pl.BlockSpec(memory_space=pl.ANY),
        scratch_shapes=[
            pltpu.VMEM((5, width, aux_dev), BF16),
            pltpu.VMEM((1, 2), BF16),
            pltpu.VMEM((1, slab), F32),
            pltpu.VMEM((1, 2), jnp.int32),
            pltpu.VMEM((5, 8, slab), F32),
            pltpu.VMEM((16, slab, slab), F32),
            pltpu.VMEM((16, slab // 2, slab), F32),
            pltpu.VMEM((16, slab // 2, slab), I16),
            pltpu.VMEM((24, 128), F32),
            pltpu.VMEM((3, 16, slab // 8, slab), I16),
            pltpu.VMEM((3, 24, 128), F32),
            pltpu.VMEM((16, slab // 8, slab), F32),
            pltpu.VMEM((16, rows, slab), F32),
            pltpu.VMEM((16, rows, slab), F32),
            pltpu.VMEM((16, rows, slab), F32),
            pltpu.VMEM((16, rows, slab), F32),
            pltpu.VMEM((16, rows, slab), F32),
            pltpu.VMEM((8, slab, width), BF16),
            pltpu.VMEM((8, slab, width), BF16),
            pltpu.VMEM((width, aux_dev), F32),
            pltpu.SemaphoreType.DMA((copies,)),
            pltpu.SemaphoreType.DMA((copies,)),
            pltpu.SemaphoreType.DMA((4,)),
            pltpu.SemaphoreType.DMA((4,)),
        ],
        compiler_params=pltpu.CompilerParams(
            collective_id=0, has_side_effects=True, vmem_limit_bytes=60 * 1024 * 1024
        ),
        cost_estimate=pl.CostEstimate(
            flops=12 * width * width * aux_dev, bytes_accessed=6 * width * aux_dev, transcendentals=0
        ),
    )(orbital_factors.reshape(width, aux_dev), occ_energy.reshape(1, 2), vir_energy.reshape(1, slab), pair_kept)
    return gamma.reshape(occ_dev, slab, aux_dev)


def solution(mesh):
    in_specs = (P("occ", None, "aux"), P("occ"), P(), P("occ", None))
    out_specs = P("occ", None, "aux")
    return jax.shard_map(
        functools.partial(on_device, mesh.shape["occ"] // 2),
        mesh=mesh, in_specs=in_specs, out_specs=out_specs, check_vma=False,
    )
```

```python
import functools

import jax
import jax.numpy as jnp
from jax import lax
from jax.experimental import pallas as pl
from jax.experimental.pallas import tpu as pltpu
from jax.sharding import PartitionSpec as P

F32 = jnp.float32
BF16 = jnp.bfloat16
I16 = jnp.int16
TOP = 32760.0
NT = (((1,), (1,)), ((), ()))

X, F, R, D, ME = range(5)
KINDS = ((ME, X), (X, F), (ME, F), (ME, R))
KX, KXF, KF, KR = range(4)
BATCHES = (
    ((KX, 0, 0), (KX, 1, 0), (KXF, 0, 0), (KF, 0, 0), (KF, 1, 0), (KR, 0, 0), (KR, 1, 0)),
    ((KX, 0, 1), (KX, 1, 1), (KXF, 0, 1), (KXF, 1, 0), (KXF, 1, 1)),
    ((KF, 0, 1), (KF, 1, 1), (KR, 0, 1), (KR, 1, 1)),
)
BLOCKS = BATCHES[0] + BATCHES[1] + BATCHES[2]
AT = {block: n for n, block in enumerate(BLOCKS)}
SPANS = ((0, 7), (7, 12), (12, 16))
TO_X = ((0, 3), (7, 12), None)
TO_F = ((2, 5), (9, 12), (12, 14))
TO_R = ((5, 7), None, (14, 16))
ORDER = (X, D, F, R)


def kernel(
    planes, b_hbm, e_hbm, v_hbm, kept_hbm, out_hbm,
    bb, e_ref, v_ref, kept_ref, small, k, rc, q, scale, ry, ry_scale, ys, rx, p, cx, cr, cf, t, tt, g,
    send, recv, local, out_sem,
):
    slab = k.shape[1]
    rows, yrows, crows = slab // 16, slab // 8, slab // 2
    half = b_hbm.shape[1] // 2

    occ, aux = lax.axis_index("occ"), lax.axis_index("aux")
    z, lo = occ // 2, lax.rem(occ, 2)
    core, y, xh = lax.rem(aux, 2), lax.rem(aux // 2, 4), aux // 8
    ahead = lax.rem(z + planes + 1 - 2 * lo, planes)
    behind = lax.rem(z + planes - 1 + 2 * lo, planes)
    occ_of = (z * 2 + 1 - lo, ahead * 2 + lo, behind * 2 + lo, behind * 2 + 1 - lo)

    def aux_of(xh_, y_, core_):
        return (xh_ * 4 + y_) * 2 + core_

    y1, y2, y3 = y + 1 - 2 * lax.rem(y, 2), lax.rem(y + 2, 4), 3 - y
    other_core, other_xh = 1 - core, 1 - xh
    to_core = (occ, aux_of(xh, y, other_core))
    to_y = [(occ, aux_of(xh, y_, core)) for y_ in (y1, y2, y3)]
    to_xh = (occ, aux_of(other_xh, y, core))
    to = [(o, aux) for o in occ_of]

    def device(where):
        return {"occ": where[0], "aux": where[1]}

    started = []
    numbers = iter(range(send.shape[0]))

    def start(src, dst, where):
        n = next(numbers)
        c = pltpu.make_async_remote_copy(
            src_ref=src, dst_ref=dst, send_sem=send.at[n], recv_sem=recv.at[n],
            device_id=device(where), device_id_type=pl.DeviceIdType.MESH,
        )
        c.start()
        started.append(c)
        return c

    own = pltpu.make_async_copy(b_hbm, bb.at[ME], local.at[0])
    own.start()
    arguments = [
        pltpu.make_async_copy(src, dst, local.at[1 + n])
        for n, (src, dst) in enumerate(((e_hbm, e_ref), (v_hbm, v_ref), (kept_hbm, kept_ref)))
    ]
    for c in arguments:
        c.start()
    barrier = pltpu.get_barrier_semaphore()
    for where in (*to, to_core, *to_y, to_xh):
        pl.semaphore_signal(barrier, inc=1, device_id=device(where), device_id_type=pl.DeviceIdType.MESH)

    pl.semaphore_wait(barrier, 9)

    mine = pl.ds(pl.multiple_of(half * (1 - lo), half), half)
    others = pl.ds(pl.multiple_of(half * lo, half), half)

    lo_mine, lo_others = half * (1 - lo), half * lo
    cut = half * 2 // 5
    rest = half - cut

    def columns_at(first_, count):
        return pl.ds(pl.multiple_of(first_, 128), count)

    def forward(slot, first_, count, where):
        c = columns_at(first_, count)
        return start(bb.at[slot, :, c], bb.at[D, :, c], to[where])

    def own_to_x(first_, count):
        c = columns_at(first_, count)
        return start(b_hbm.at[:, c], bb.at[X, :, c], to[X])

    first = []
    for o in range(2):
        r = slice(o * slab, (o + 1) * slab)
        first.append((
            start(b_hbm.at[r, others], bb.at[X, r, others], to[X]),
            start(b_hbm.at[r, mine], bb.at[F, r, mine], to[R]),
            start(b_hbm.at[r, others], bb.at[R, r, others], to[F]),
        ))
    second = [
        own_to_x(lo_mine, rest),
        start(b_hbm.at[:, others], bb.at[F, :, others], to[R]),
        start(b_hbm.at[:, mine], bb.at[R, :, mine], to[F]),
    ]

    for c in arguments:
        c.wait()
    for i in range(2):
        small[ME, i:i + 1] = jnp.broadcast_to(e_ref[:, i:i + 1].astype(F32), (1, slab))
        small[ME, 2 + i:3 + i] = jnp.broadcast_to(kept_ref[:, i:i + 1].astype(F32), (1, slab))
    small[ME, 4:8] = jnp.zeros((4, slab), F32)
    my_row = core * crows + y * yrows + xh * rows
    spot = lax.broadcasted_iota(jnp.int32, (rows, slab), 1) - lax.broadcasted_iota(jnp.int32, (rows, slab), 0)
    mine_v = jnp.sum(jnp.where(spot == my_row, v_ref[...], 0.0), axis=1, keepdims=True)
    virtual = mine_v + v_ref[...]

    smalls = [
        start(small.at[ME], small.at[slot], to[back])
        for slot, back in ((X, X), (F, R), (R, F), (D, D))
    ]

    def pair_sums(lo_, hi_):
        for n in range(lo_, hi_):
            kind, u, v = BLOCKS[n]
            one, two = KINDS[kind]
            swap = 1 - lo if kind == KR else lo
            columns = others if kind == KR else mine
            head, tail = one + swap * (two - one), two + swap * (one - two)
            a_at = pl.multiple_of((u + swap * (v - u)) * slab, slab)
            b_at = pl.multiple_of((v + swap * (u - v)) * slab, slab)
            a = bb[head, pl.ds(a_at, slab), columns]
            b = bb[tail, pl.ds(b_at, slab), columns]
            direct = lax.dot_general(a + a, b, NT, preferred_element_type=F32)
            exchanged = lax.dot_general(b, a, NT, preferred_element_type=F32)
            k[n] = direct - exchanged

    my_half = pl.ds(pl.multiple_of(core * crows, crows), crows)
    its_half = pl.ds(pl.multiple_of(other_core * crows, crows), crows)

    def to_other_core(lo_, hi_):
        return start(k.at[lo_:hi_, its_half], rc.at[lo_:hi_], to_core)

    def sum_cores(batch, lo_, hi_):
        for n in range(lo_, hi_):
            total = k[n, my_half] + rc[n]
            k[n, my_half] = total
            top = jnp.max(jnp.max(jnp.abs(total), axis=0, keepdims=True), axis=1, keepdims=True)
            top = jnp.maximum(top, 1e-30)
            q[n] = jnp.round(total * (TOP / top)).astype(jnp.int32).astype(I16)
            row = 8 * batch + n - SPANS[batch][0]
            scale[row:row + 1] = jnp.broadcast_to(top * (1.0 / TOP), (1, 128))

    def along_y(batch):
        lo_, hi_ = SPANS[batch]
        s = slice(8 * batch, 8 * batch + 8)
        out = []
        for j, y_ in enumerate((y1, y2, y3)):
            r = pl.ds(pl.multiple_of(y_ * yrows, yrows), yrows)
            out.append(start(scale.at[s], ry_scale.at[j, s], to_y[j]))
            out.append(start(q.at[lo_:hi_, r], ry.at[j, lo_:hi_], to_y[j]))
        return out

    def sum_y(batch, copies):
        for c in copies:
            c.wait_recv()
        lo_, hi_ = SPANS[batch]
        r = pl.ds(pl.multiple_of(core * crows + y * yrows, yrows), yrows)
        for n in range(lo_, hi_):
            row = 8 * batch + n - lo_
            total = k[n, r]
            for j in range(3):
                total += ry[j, n].astype(jnp.int32).astype(F32) * ry_scale[j, row:row + 1, 0:1]
            ys[n] = total
        x_rows = pl.ds(pl.multiple_of(other_xh * rows, rows), rows)
        return start(ys.at[lo_:hi_, x_rows], rx.at[lo_:hi_], to_xh)

    def sum_x(batch, c):
        c.wait_recv()
        lo_, hi_ = SPANS[batch]
        p[lo_:hi_] = ys[lo_:hi_, pl.ds(pl.multiple_of(xh * rows, rows), rows)] + rx[lo_:hi_]
        out = []
        for span, dst, where in ((TO_X[batch], cx, to[X]), (TO_F[batch], cr, to[F]), (TO_R[batch], cf, to[R])):
            if span is not None:
                out.append(start(p.at[slice(*span)], dst.at[slice(*span)], where))
        return out

    own.wait()
    for c in first[0]:
        c.wait_recv()
    pair_sums(0, 3)
    core0 = [to_other_core(0, 3)]
    pair_sums(3, 7)
    core0.append(to_other_core(3, 7))
    core0[0].wait_recv()
    sum_cores(0, 0, 3)
    core0[1].wait_recv()
    sum_cores(0, 3, 7)
    y_0 = along_y(0)
    for c in first[1]:
        c.wait_recv()
    pair_sums(*SPANS[1])
    core1 = to_other_core(*SPANS[1])
    pair_sums(*SPANS[2])
    core2 = to_other_core(*SPANS[2])
    core1.wait_recv()
    sum_cores(1, *SPANS[1])
    y_1 = along_y(1)
    core2.wait_recv()
    sum_cores(2, *SPANS[2])
    y_2 = along_y(2)
    diagonal = [forward(X, lo_mine, cut, F)]
    x_0 = sum_y(0, y_0)
    x_1 = sum_y(1, y_1)
    place_0 = sum_x(0, x_0)
    x_2 = sum_y(2, y_2)
    place_1 = sum_x(1, x_1)
    second.append(own_to_x(lo_mine + rest, cut))
    place_2 = sum_x(2, x_2)
    second[0].wait_recv()
    diagonal += [forward(X, lo_mine + cut, rest, F), forward(X, lo_others, cut, F)]

    my_rows = pl.ds(pl.multiple_of(my_row, rows), rows)

    def finish(pair):
        swap = lo if pair in (X, F) else 1 - lo
        flag_row = 2 if pair in (X, D) else 3
        flag = small[ME + swap * (pair - ME), flag_row:flag_row + 1]
        for i in range(2):
            for j in range(2):
                if pair == X:
                    total = p[AT[KX, i, j]] + cx[AT[KX, j, i]]
                elif pair == F:
                    total = p[AT[KF, i, j]] + cf[AT[KR, j, i]]
                elif pair == R:
                    total = p[AT[KR, i, j]] + cr[AT[KF, j, i]]
                else:
                    total = cx[AT[KXF, i, j]] + cr[AT[KXF, j, i]]
                energy = small[ME, i:i + 1] + small[pair, j:j + 1]
                row = 2 * ORDER.index(pair) + i
                t[row, my_rows, j * slab:(j + 1) * slab] = (flag * total / (energy - virtual)).astype(BF16)

    def spread(part, core_, y_, xh_, where):
        r = pl.ds(pl.multiple_of(core_ * crows + y_ * yrows + xh_ * rows, rows), rows)
        source = t.at[4 * part:4 * part + 4, r]
        return start(source, source, where)

    own_part, near, far = [], [], [[], []]
    for c in smalls + place_0 + place_1:
        c.wait_recv()
    for h in range(2):
        if h == 1:
            for c in place_2:
                c.wait_recv()
        finish(ORDER[2 * h])
        finish(ORDER[2 * h + 1])
        own_part.append([spread(h, core, y, xh, where) for where in (to_xh, to_core, to_y[1], to_y[0], to_y[2])])
    for h in range(2):
        own_part[h][0].wait_recv()
        near.append([spread(h, core, y, other_xh, where) for where in (to_core, to_y[1], to_y[0], to_y[2])])
    diagonal.append(forward(F, lo_mine + cut, rest, X))
    for copies, skip, xh_ in ((own_part, 2, xh), (near, 1, other_xh)):
        for h in range(2):
            for c, y_ in ((copies[h][skip + 1], y1), (copies[h][skip + 2], y3), (copies[h][skip], y2)):
                c.wait_recv()
                far[h].append(spread(h, core, y_, xh_, to_core))

    def orient(h):
        for c in (own_part[h][1], near[h][0], *far[h]):
            c.wait_recv()

        for n in range(4 * h, 4 * h + 4):
            second_at = 1 if ORDER[n // 2] in (X, F) else 0

            @pl.when(lo != second_at)
            def _(n=n):
                tt[n] = t[n]

            @pl.when(lo == second_at)
            def _(n=n):
                for j in range(2):
                    tt[n, :, j * slab:(j + 1) * slab] = t[n, :, j * slab:(j + 1) * slab].T

    pieces = ((lo_mine, cut), (lo_mine + cut, rest), (lo_others, cut), (lo_others + cut, rest))

    def apply(slots, piece, earlier):
        c = columns_at(*piece)
        out = []
        for i in range(2):
            total = earlier(i)
            for slot in slots:
                term = jnp.dot(tt[2 * ORDER.index(slot) + i], bb[slot, :, c], preferred_element_type=F32)
                total = term if total is None else total + term
            out.append(total)
        return out

    orient(0)
    second[3].wait_recv()
    at = 0
    for n, piece in enumerate(pieces):
        if n < 2:
            diagonal[n].wait_recv()
        for i, total in enumerate(apply((X, D) if n < 2 else (X,), piece, lambda i: None)):
            g[i * slab:(i + 1) * slab, at:at + piece[1]] = total
        at += piece[1]
    orient(1)
    second[1].wait_recv()
    second[2].wait_recv()
    at = 0
    results = []
    for n, piece in enumerate(pieces):
        here = slice(at, at + piece[1])
        if n >= 2:
            diagonal[n].wait_recv()
        slots = (F, R) if n < 2 else (F, R, D)
        for i, total in enumerate(apply(slots, piece, lambda i: g[i * slab:(i + 1) * slab, here])):
            g[i * slab:(i + 1) * slab, here] = total
        result = pltpu.make_async_copy(g.at[:, here], out_hbm.at[:, columns_at(*piece)], out_sem.at[n])
        result.start()
        results.append(result)
        at += piece[1]
    for c in started:
        c.wait_send()
    for c in results:
        c.wait()


def on_device(planes, orbital_factors, occ_energy, vir_energy, pair_kept):
    occ_dev, slab, aux_dev = orbital_factors.shape
    width = occ_dev * slab
    rows = slab // 16
    copies = 80
    gamma = pl.pallas_call(
        functools.partial(kernel, planes),
        out_shape=jax.ShapeDtypeStruct((width, aux_dev), F32),
        in_specs=[pl.BlockSpec(memory_space=pl.ANY)] * 4,
        out_specs=pl.BlockSpec(memory_space=pl.ANY),
        scratch_shapes=[
            pltpu.VMEM((5, width, aux_dev), BF16),
            pltpu.VMEM((1, 2), BF16),
            pltpu.VMEM((1, slab), F32),
            pltpu.VMEM((1, 2), jnp.int32),
            pltpu.VMEM((5, 8, slab), F32),
            pltpu.VMEM((16, slab, slab), F32),
            pltpu.VMEM((16, slab // 2, slab), F32),
            pltpu.VMEM((16, slab // 2, slab), I16),
            pltpu.VMEM((24, 128), F32),
            pltpu.VMEM((3, 16, slab // 8, slab), I16),
            pltpu.VMEM((3, 24, 128), F32),
            pltpu.VMEM((16, slab // 8, slab), F32),
            pltpu.VMEM((16, rows, slab), F32),
            pltpu.VMEM((16, rows, slab), F32),
            pltpu.VMEM((16, rows, slab), F32),
            pltpu.VMEM((16, rows, slab), F32),
            pltpu.VMEM((16, rows, slab), F32),
            pltpu.VMEM((8, slab, width), BF16),
            pltpu.VMEM((8, slab, width), BF16),
            pltpu.VMEM((width, aux_dev), F32),
            pltpu.SemaphoreType.DMA((copies,)),
            pltpu.SemaphoreType.DMA((copies,)),
            pltpu.SemaphoreType.DMA((4,)),
            pltpu.SemaphoreType.DMA((4,)),
        ],
        compiler_params=pltpu.CompilerParams(
            collective_id=0, has_side_effects=True, vmem_limit_bytes=60 * 1024 * 1024
        ),
        cost_estimate=pl.CostEstimate(
            flops=12 * width * width * aux_dev, bytes_accessed=6 * width * aux_dev, transcendentals=0
        ),
    )(orbital_factors.reshape(width, aux_dev), occ_energy.reshape(1, 2), vir_energy.reshape(1, slab), pair_kept)
    return gamma.reshape(occ_dev, slab, aux_dev)


def solution(mesh):
    in_specs = (P("occ", None, "aux"), P("occ"), P(), P("occ", None))
    out_specs = P("occ", None, "aux")
    return jax.shard_map(
        functools.partial(on_device, mesh.shape["occ"] // 2),
        mesh=mesh, in_specs=in_specs, out_specs=out_specs, check_vma=False,
    )
```

```python
import functools

import jax
import jax.numpy as jnp
from jax import lax
from jax.experimental import pallas as pl
from jax.experimental.pallas import tpu as pltpu
from jax.sharding import PartitionSpec as P

F32 = jnp.float32
BF16 = jnp.bfloat16
I16 = jnp.int16
TOP = 32760.0
NT = (((1,), (1,)), ((), ()))

X, F, R, D, ME = range(5)
KINDS = ((ME, X), (X, F), (ME, F), (ME, R))
KX, KXF, KF, KR = range(4)
BATCHES = (
    ((KX, 0, 0), (KX, 1, 0), (KXF, 0, 0), (KF, 0, 0), (KF, 1, 0), (KR, 0, 0), (KR, 1, 0)),
    ((KX, 0, 1), (KX, 1, 1), (KXF, 0, 1), (KXF, 1, 0), (KXF, 1, 1)),
    ((KF, 0, 1), (KF, 1, 1), (KR, 0, 1), (KR, 1, 1)),
)
BLOCKS = BATCHES[0] + BATCHES[1] + BATCHES[2]
AT = {block: n for n, block in enumerate(BLOCKS)}
SPANS = ((0, 7), (7, 12), (12, 16))
TO_X = ((0, 3), (7, 12), None)
TO_F = ((2, 5), (9, 12), (12, 14))
TO_R = ((5, 7), None, (14, 16))
ORDER = (X, D, F, R)


def kernel(
    planes, b_hbm, e_hbm, v_hbm, kept_hbm, out_hbm,
    bb, e_ref, v_ref, kept_ref, small, k, rc, q, scale, ry, ry_scale, ys, rx, p, cx, cr, cf, t, tt, g,
    send, recv, local, out_sem,
):
    slab = k.shape[1]
    rows, yrows, crows = slab // 16, slab // 8, slab // 2
    half = b_hbm.shape[1] // 2

    occ, aux = lax.axis_index("occ"), lax.axis_index("aux")
    z, lo = occ // 2, lax.rem(occ, 2)
    core, y, xh = lax.rem(aux, 2), lax.rem(aux // 2, 4), aux // 8
    ahead = lax.rem(z + planes + 1 - 2 * lo, planes)
    behind = lax.rem(z + planes - 1 + 2 * lo, planes)
    occ_of = (z * 2 + 1 - lo, ahead * 2 + lo, behind * 2 + lo, behind * 2 + 1 - lo)

    def aux_of(xh_, y_, core_):
        return (xh_ * 4 + y_) * 2 + core_

    y1, y2, y3 = y + 1 - 2 * lax.rem(y, 2), lax.rem(y + 2, 4), 3 - y
    other_core, other_xh = 1 - core, 1 - xh
    to_core = (occ, aux_of(xh, y, other_core))
    to_y = [(occ, aux_of(xh, y_, core)) for y_ in (y1, y2, y3)]
    to_xh = (occ, aux_of(other_xh, y, core))
    to = [(o, aux) for o in occ_of]

    def device(where):
        return {"occ": where[0], "aux": where[1]}

    started = []
    numbers = iter(range(send.shape[0]))

    def start(src, dst, where):
        n = next(numbers)
        c = pltpu.make_async_remote_copy(
            src_ref=src, dst_ref=dst, send_sem=send.at[n], recv_sem=recv.at[n],
            device_id=device(where), device_id_type=pl.DeviceIdType.MESH,
        )
        c.start()
        started.append(c)
        return c

    own = pltpu.make_async_copy(b_hbm, bb.at[ME], local.at[0])
    own.start()
    arguments = [
        pltpu.make_async_copy(src, dst, local.at[1 + n])
        for n, (src, dst) in enumerate(((e_hbm, e_ref), (v_hbm, v_ref), (kept_hbm, kept_ref)))
    ]
    for c in arguments:
        c.start()
    barrier = pltpu.get_barrier_semaphore()
    for where in (*to, to_core, *to_y, to_xh):
        pl.semaphore_signal(barrier, inc=1, device_id=device(where), device_id_type=pl.DeviceIdType.MESH)

    pl.semaphore_wait(barrier, 9)

    mine = pl.ds(pl.multiple_of(half * (1 - lo), half), half)
    others = pl.ds(pl.multiple_of(half * lo, half), half)

    lo_mine, lo_others = half * (1 - lo), half * lo
    cut = half * 2 // 5
    rest = half - cut

    def columns_at(first_, count):
        return pl.ds(pl.multiple_of(first_, 128), count)

    def forward(slot, first_, count, where):
        c = columns_at(first_, count)
        return start(bb.at[slot, :, c], bb.at[D, :, c], to[where])

    def own_to_x(first_, count):
        c = columns_at(first_, count)
        return start(b_hbm.at[:, c], bb.at[X, :, c], to[X])

    first = []
    for o in range(2):
        r = slice(o * slab, (o + 1) * slab)
        first.append((
            start(b_hbm.at[r, others], bb.at[X, r, others], to[X]),
            start(b_hbm.at[r, mine], bb.at[F, r, mine], to[R]),
            start(b_hbm.at[r, others], bb.at[R, r, others], to[F]),
        ))
    second = [
        own_to_x(lo_mine, rest),
        start(b_hbm.at[:, others], bb.at[F, :, others], to[R]),
        start(b_hbm.at[:, mine], bb.at[R, :, mine], to[F]),
    ]

    for c in arguments:
        c.wait()
    for i in range(2):
        small[ME, i:i + 1] = jnp.broadcast_to(e_ref[:, i:i + 1].astype(F32), (1, slab))
        small[ME, 2 + i:3 + i] = jnp.broadcast_to(kept_ref[:, i:i + 1].astype(F32), (1, slab))
    small[ME, 4:8] = jnp.zeros((4, slab), F32)
    my_row = core * crows + y * yrows + xh * rows
    spot = lax.broadcasted_iota(jnp.int32, (rows, slab), 1) - lax.broadcasted_iota(jnp.int32, (rows, slab), 0)
    mine_v = jnp.sum(jnp.where(spot == my_row, v_ref[...], 0.0), axis=1, keepdims=True)
    virtual = mine_v + v_ref[...]

    smalls = [
        start(small.at[ME], small.at[slot], to[back])
        for slot, back in ((X, X), (F, R), (R, F), (D, D))
    ]

    def pair_sums(lo_, hi_):
        for n in range(lo_, hi_):
            kind, u, v = BLOCKS[n]
            one, two = KINDS[kind]
            swap = 1 - lo if kind == KR else lo
            columns = others if kind == KR else mine
            head, tail = one + swap * (two - one), two + swap * (one - two)
            a_at = pl.multiple_of((u + swap * (v - u)) * slab, slab)
            b_at = pl.multiple_of((v + swap * (u - v)) * slab, slab)
            a = bb[head, pl.ds(a_at, slab), columns]
            b = bb[tail, pl.ds(b_at, slab), columns]
            direct = lax.dot_general(a + a, b, NT, preferred_element_type=F32)
            exchanged = lax.dot_general(b, a, NT, preferred_element_type=F32)
            k[n] = direct - exchanged

    my_half = pl.ds(pl.multiple_of(core * crows, crows), crows)
    its_half = pl.ds(pl.multiple_of(other_core * crows, crows), crows)

    def to_other_core(lo_, hi_):
        return start(k.at[lo_:hi_, its_half], rc.at[lo_:hi_], to_core)

    def sum_cores(batch, lo_, hi_):
        for n in range(lo_, hi_):
            total = k[n, my_half] + rc[n]
            k[n, my_half] = total
            top = jnp.max(jnp.max(jnp.abs(total), axis=0, keepdims=True), axis=1, keepdims=True)
            top = jnp.maximum(top, 1e-30)
            q[n] = jnp.round(total * (TOP / top)).astype(jnp.int32).astype(I16)
            row = 8 * batch + n - SPANS[batch][0]
            scale[row:row + 1] = jnp.broadcast_to(top * (1.0 / TOP), (1, 128))

    def along_y(batch):
        lo_, hi_ = SPANS[batch]
        s = slice(8 * batch, 8 * batch + 8)
        out = []
        for j, y_ in enumerate((y1, y2, y3)):
            r = pl.ds(pl.multiple_of(y_ * yrows, yrows), yrows)
            out.append(start(scale.at[s], ry_scale.at[j, s], to_y[j]))
            out.append(start(q.at[lo_:hi_, r], ry.at[j, lo_:hi_], to_y[j]))
        return out

    def sum_y(batch, copies):
        for c in copies:
            c.wait_recv()
        lo_, hi_ = SPANS[batch]
        r = pl.ds(pl.multiple_of(core * crows + y * yrows, yrows), yrows)
        for n in range(lo_, hi_):
            row = 8 * batch + n - lo_
            total = k[n, r]
            for j in range(3):
                total += ry[j, n].astype(jnp.int32).astype(F32) * ry_scale[j, row:row + 1, 0:1]
            ys[n] = total
        x_rows = pl.ds(pl.multiple_of(other_xh * rows, rows), rows)
        return start(ys.at[lo_:hi_, x_rows], rx.at[lo_:hi_], to_xh)

    def sum_x(batch, c):
        c.wait_recv()
        lo_, hi_ = SPANS[batch]
        p[lo_:hi_] = ys[lo_:hi_, pl.ds(pl.multiple_of(xh * rows, rows), rows)] + rx[lo_:hi_]
        out = []
        for span, dst, where in ((TO_X[batch], cx, to[X]), (TO_F[batch], cr, to[F]), (TO_R[batch], cf, to[R])):
            if span is not None:
                out.append(start(p.at[slice(*span)], dst.at[slice(*span)], where))
        return out

    own.wait()
    for c in first[0]:
        c.wait_recv()
    pair_sums(0, 3)
    core0 = [to_other_core(0, 3)]
    pair_sums(3, 7)
    core0.append(to_other_core(3, 7))
    core0[0].wait_recv()
    sum_cores(0, 0, 3)
    core0[1].wait_recv()
    sum_cores(0, 3, 7)
    y_0 = along_y(0)
    for c in first[1]:
        c.wait_recv()
    pair_sums(*SPANS[1])
    core1 = to_other_core(*SPANS[1])
    pair_sums(*SPANS[2])
    core2 = to_other_core(*SPANS[2])
    core1.wait_recv()
    sum_cores(1, *SPANS[1])
    y_1 = along_y(1)
    core2.wait_recv()
    sum_cores(2, *SPANS[2])
    y_2 = along_y(2)
    diagonal = [forward(X, lo_mine, cut, F)]
    x_0 = sum_y(0, y_0)
    x_1 = sum_y(1, y_1)
    place_0 = sum_x(0, x_0)
    x_2 = sum_y(2, y_2)
    place_1 = sum_x(1, x_1)
    second.append(own_to_x(lo_mine + rest, cut))
    place_2 = sum_x(2, x_2)
    second[0].wait_recv()
    diagonal += [forward(X, lo_mine + cut, rest, F), forward(X, lo_others, cut, F)]

    my_rows = pl.ds(pl.multiple_of(my_row, rows), rows)

    def finish(pair):
        swap = lo if pair in (X, F) else 1 - lo
        flag_row = 2 if pair in (X, D) else 3
        flag = small[ME + swap * (pair - ME), flag_row:flag_row + 1]
        for i in range(2):
            for j in range(2):
                if pair == X:
                    total = p[AT[KX, i, j]] + cx[AT[KX, j, i]]
                elif pair == F:
                    total = p[AT[KF, i, j]] + cf[AT[KR, j, i]]
                elif pair == R:
                    total = p[AT[KR, i, j]] + cr[AT[KF, j, i]]
                else:
                    total = cx[AT[KXF, i, j]] + cr[AT[KXF, j, i]]
                energy = small[ME, i:i + 1] + small[pair, j:j + 1]
                row = 2 * ORDER.index(pair) + i
                t[row, my_rows, j * slab:(j + 1) * slab] = (flag * total / (energy - virtual)).astype(BF16)

    def spread(part, core_, y_, xh_, where):
        r = pl.ds(pl.multiple_of(core_ * crows + y_ * yrows + xh_ * rows, rows), rows)
        source = t.at[4 * part:4 * part + 4, r]
        return start(source, source, where)

    own_part, near, far = [], [], [[], []]
    for c in smalls + place_0 + place_1:
        c.wait_recv()
    for h in range(2):
        if h == 1:
            for c in place_2:
                c.wait_recv()
        finish(ORDER[2 * h])
        finish(ORDER[2 * h + 1])
        own_part.append([spread(h, core, y, xh, where) for where in (to_xh, to_core, to_y[1], to_y[0], to_y[2])])
    for h in range(2):
        own_part[h][0].wait_recv()
        near.append([spread(h, core, y, other_xh, where) for where in (to_core, to_y[1], to_y[0], to_y[2])])
    diagonal.append(forward(F, lo_mine + cut, rest, X))
    for copies, skip, xh_ in ((own_part, 2, xh), (near, 1, other_xh)):
        for h in range(2):
            for c, y_ in ((copies[h][skip + 1], y1), (copies[h][skip + 2], y3), (copies[h][skip], y2)):
                c.wait_recv()
                far[h].append(spread(h, core, y_, xh_, to_core))

    def orient(h):
        for c in (own_part[h][1], near[h][0], *far[h]):
            c.wait_recv()

        for n in range(4 * h, 4 * h + 4):
            second_at = 1 if ORDER[n // 2] in (X, F) else 0

            @pl.when(lo != second_at)
            def _(n=n):
                tt[n] = t[n]

            @pl.when(lo == second_at)
            def _(n=n):
                for j in range(2):
                    tt[n, :, j * slab:(j + 1) * slab] = t[n, :, j * slab:(j + 1) * slab].T

    pieces = ((lo_mine, cut), (lo_mine + cut, rest), (lo_others, cut), (lo_others + cut, rest))

    def apply(slots, piece, i, total):
        c = columns_at(*piece)
        for slot in slots:
            term = jnp.dot(tt[2 * ORDER.index(slot) + i], bb[slot, :, c], preferred_element_type=F32)
            total = term if total is None else total + term
        return total

    orient(0)
    second[3].wait_recv()
    at = 0
    for n, piece in enumerate(pieces):
        if n < 2:
            diagonal[n].wait_recv()
        for i in range(2):
            g[i * slab:(i + 1) * slab, at:at + piece[1]] = apply((X, D) if n < 2 else (X,), piece, i, None)
        at += piece[1]
    orient(1)
    second[1].wait_recv()
    second[2].wait_recv()
    at = 0
    results = []
    for n, piece in enumerate(pieces):
        here = slice(at, at + piece[1])
        if n >= 2:
            diagonal[n].wait_recv()
        slots = (F, R) if n < 2 else (F, R, D)
        for i in range(2):
            r = slice(i * slab, (i + 1) * slab)
            g[r, here] = apply(slots, piece, i, g[r, here])
            result = pltpu.make_async_copy(g.at[r, here], out_hbm.at[r, columns_at(*piece)], out_sem.at[2 * n + i])
            result.start()
            results.append(result)
        at += piece[1]
    for c in started:
        c.wait_send()
    for c in results:
        c.wait()


def on_device(planes, orbital_factors, occ_energy, vir_energy, pair_kept):
    occ_dev, slab, aux_dev = orbital_factors.shape
    width = occ_dev * slab
    rows = slab // 16
    copies = 80
    gamma = pl.pallas_call(
        functools.partial(kernel, planes),
        out_shape=jax.ShapeDtypeStruct((width, aux_dev), F32),
        in_specs=[pl.BlockSpec(memory_space=pl.ANY)] * 4,
        out_specs=pl.BlockSpec(memory_space=pl.ANY),
        scratch_shapes=[
            pltpu.VMEM((5, width, aux_dev), BF16),
            pltpu.VMEM((1, 2), BF16),
            pltpu.VMEM((1, slab), F32),
            pltpu.VMEM((1, 2), jnp.int32),
            pltpu.VMEM((5, 8, slab), F32),
            pltpu.VMEM((16, slab, slab), F32),
            pltpu.VMEM((16, slab // 2, slab), F32),
            pltpu.VMEM((16, slab // 2, slab), I16),
            pltpu.VMEM((24, 128), F32),
            pltpu.VMEM((3, 16, slab // 8, slab), I16),
            pltpu.VMEM((3, 24, 128), F32),
            pltpu.VMEM((16, slab // 8, slab), F32),
            pltpu.VMEM((16, rows, slab), F32),
            pltpu.VMEM((16, rows, slab), F32),
            pltpu.VMEM((16, rows, slab), F32),
            pltpu.VMEM((16, rows, slab), F32),
            pltpu.VMEM((16, rows, slab), F32),
            pltpu.VMEM((8, slab, width), BF16),
            pltpu.VMEM((8, slab, width), BF16),
            pltpu.VMEM((width, aux_dev), F32),
            pltpu.SemaphoreType.DMA((copies,)),
            pltpu.SemaphoreType.DMA((copies,)),
            pltpu.SemaphoreType.DMA((4,)),
            pltpu.SemaphoreType.DMA((8,)),
        ],
        compiler_params=pltpu.CompilerParams(
            collective_id=0, has_side_effects=True, vmem_limit_bytes=60 * 1024 * 1024
        ),
        cost_estimate=pl.CostEstimate(
            flops=12 * width * width * aux_dev, bytes_accessed=6 * width * aux_dev, transcendentals=0
        ),
    )(orbital_factors.reshape(width, aux_dev), occ_energy.reshape(1, 2), vir_energy.reshape(1, slab), pair_kept)
    return gamma.reshape(occ_dev, slab, aux_dev)


def solution(mesh):
    in_specs = (P("occ", None, "aux"), P("occ"), P(), P("occ", None))
    out_specs = P("occ", None, "aux")
    return jax.shard_map(
        functools.partial(on_device, mesh.shape["occ"] // 2),
        mesh=mesh, in_specs=in_specs, out_specs=out_specs, check_vma=False,
    )
```
